32 devices in a mesh: groups: 2 (over x), tok: 16 (over z, y, core).
Axes of the slice: x: 2, y: 2, z: 4, core: 2. Of those that a mesh axis runs over, the one named last changes fastest.
Arguments:
- activations: bfloat16 [4096, 4096], P(('groups', 'tok')), parts along dimension 0, may hold values from -6 to 6
- out_grads: bfloat16 [4096, 14336], P(('groups', 'tok')), parts along dimension 0, may hold values from -6 to 6
- query_grad: bfloat16 [8192, 14336], P(('groups', 'tok')), parts along dimension 0, may hold values from -0.00024414062 to 0.00024414062
- token_order: int32 [4096], P('groups'), parts along dimension 0, may hold values from 0 to 2047, each once
- doc_ids: int32 [4096], P('groups'), parts along dimension 0, may hold values from 0 to 31, never falling along the last dimension, each value on 1 to 128 neighbouring positions
Outputs:
- scores: float32 [64], P(('groups', 'tok')), parts along dimension 0
The draws below stay inside these ranges and needn't reach their ends.
There are 2 independent parts, one for each index of `groups`. The reference program is written for one: setup_inputs(seed, part) draws one part's arguments, and reference() takes and returns one part's arrays. A program takes and returns all parts, laid end to end along the dimension named above; each array names one. Nothing has to cross between parts.
All inputs are finite; a program needn't handle non-finite values.
Results may differ from the reference program's by a relative error of at most 0.0003.
Values may be sent and summed in bfloat16 or wider, within the bound.
A program may use at most 128 MiB of HBM per device.

```python
import math
import jax
import jax.numpy as jnp
import numpy as np
from jax import lax

D_IN = 4096
D_OUT = 14336
TOK_DEV = 128
E_DEV = 2
TOKENS = 2048
EXAMPLES = 32
N_TOK = 16


def steps_of(key, extent, pieces, smallest, high):
    loudness = 1.0
    for axis_at, shards_of in pieces:
        draws = jax.random.uniform(jax.random.fold_in(jax.random.fold_in(key, 6), axis_at), (shards_of,), jnp.float32, smallest / len(pieces), high / len(pieces))
        loudness = loudness * jnp.repeat(jnp.exp(draws), extent[axis_at] // shards_of).reshape((-1,) + (1,) * (len(extent) - 1 - axis_at))
    return loudness


def length_profile(number_of, total, bound, lean):
    weights = [(1 << 20) // math.isqrt(standing ** lean) + 1 for standing in range(2, number_of + 1)]
    rest, holding = total - bound - (number_of - 1), [1] * (number_of - 1)
    while rest > 0:
        free = [i for i in range(number_of - 1) if holding[i] < bound]
        mass, remaining = sum([weights[i] for i in free]), rest
        for i in free:
            addition = min(bound - holding[i], max(1, remaining * weights[i] // mass), rest)
            holding[i] = holding[i] + addition
            rest = rest - addition
    return np.array([bound] + holding)


def ragged(rng, number_of, total, limit, slope):
    if number_of == 2:
        one = jax.random.randint(rng, (), max(1, total - limit), min(limit, total - 1) + 1)
        return jnp.stack([one, total - one])
    tallies = jnp.asarray(length_profile(number_of, total, limit, slope), jnp.int32)
    twos = (number_of - 1) // 2
    source_of, taker = tallies[1:1 + 2 * twos:2], tallies[2:2 + 2 * twos:2]
    slack = jnp.minimum(source_of - 1, limit - taker)
    passed = jax.random.randint(jax.random.fold_in(rng, 1), (twos,), 0, 1 << 20) % (slack + 1)
    tallies = tallies.at[1:1 + 2 * twos:2].set(source_of - passed).at[2:2 + 2 * twos:2].set(taker + passed)
    return tallies[jax.random.permutation(jax.random.fold_in(rng, 2), number_of)]


def bell_draw(own_key, dims, spread, bound, split=(), kind=jnp.bfloat16):
    entries = spread * jax.random.normal(own_key, dims, jnp.float32)
    if split:
        entries = entries * steps_of(own_key, dims, split, -0.22, 0.18)
    return jnp.clip(entries, -bound, bound).astype(kind)


def setup_inputs(seed: int = 0, part: int = 0) -> dict:
    arg_keys = jax.random.split(jax.random.key(seed), 6)
    part_keys = jax.random.split(jax.random.fold_in(arg_keys[5], part), 6)
    return {
        "activations": bell_draw(part_keys[0], (TOKENS, D_IN), 1.0, 6.0, ((0, 16),)),
        "out_grads": bell_draw(part_keys[1], (TOKENS, D_OUT), 1.0, 6.0, ((0, 16),)),
        "query_grad": bell_draw(part_keys[2], (D_IN, D_OUT), (8 * D_IN * D_OUT) ** -0.5, 0.00024414062, ((0, 16),)),
        "token_order": jax.random.permutation(part_keys[3], TOKENS).astype(jnp.int32),
        "doc_ids": jnp.searchsorted(jnp.cumsum(ragged(part_keys[4], EXAMPLES, TOKENS, 2 * TOK_DEV // E_DEV, 1)), jnp.arange(TOKENS), side="right").astype(jnp.int32),
    }


def reference(activations, out_grads, query_grad, token_order, doc_ids):
    def score_block(operands):
        rows_in, grads_in = operands
        projected = jnp.dot(rows_in, query_grad, preferred_element_type=jnp.float32)
        return jnp.sum(projected * grads_in.astype(jnp.float32), axis=1)

    token_scores = lax.map(score_block, (activations.reshape(N_TOK, TOK_DEV, D_IN), out_grads.reshape(N_TOK, TOK_DEV, D_OUT)))
    example_of = jnp.take(doc_ids, token_order)
    return jax.ops.segment_sum(token_scores.reshape(TOKENS), example_of, num_segments=EXAMPLES)
```

```python
import functools

import jax
import jax.numpy as jnp
from jax import lax
from jax.experimental import pallas as pl
from jax.experimental.pallas import tpu as pltpu
from jax.sharding import PartitionSpec as P

E_DEV = 2
ROW = 4
LINE = 4
MESH = pl.DeviceIdType.MESH
NEED = ((0,), (0, 1), (2, 3), (3,))
RIGHTWARD = {1: (0, 1, 2, 3), 2: (2, 3), 3: (3,)}
LEFTWARD = {2: (0, 1, 2, 3), 1: (0, 1), 0: (0,)}


def exchange(
    near, act, grads, query, g_all, a_all, q_own, q_next,
    g_recv, a_recv, q_recv, n_recv, row_send, right_a, right_b, left_a, left_b, act_right, act_left,
    act_row, q_send,
):
    me = lax.axis_index("tok")
    z = me // ROW
    s = me % ROW
    y, c = s // 2, s % 2
    tokens, features = act.shape
    q_rows = query.shape[0]
    width = g_all.shape[1]
    far = width - near
    block = features // LINE
    core_peer = y * 2 + 1 - c
    y_peer = (1 - y) * 2 + c
    diagonal = (1 - y) * 2 + 1 - c
    peers = (s, core_peer, y_peer, diagonal)

    barrier = pltpu.get_barrier_semaphore()
    for step in range(1, ROW * LINE):
        other = (me + step) % (ROW * LINE)
        pl.semaphore_signal(barrier, inc=1, device_id={"tok": other}, device_id_type=MESH)
    pl.semaphore_wait(barrier, ROW * LINE - 1)

    def remote(source, target, send, recv, line, quarter):
        return pltpu.make_async_remote_copy(
            src_ref=source, dst_ref=target, send_sem=send, recv_sem=recv,
            device_id={"tok": line * ROW + quarter}, device_id_type=MESH,
        )

    def rows(line, quarter):
        return pl.ds(pl.multiple_of((line * ROW + quarter) * tokens, tokens), tokens)

    def g_piece(line, quarter, piece):
        columns = pl.ds(0, near) if piece == 0 else pl.ds(near, far)
        return g_all.at[rows(line, quarter), columns]

    def a_piece(line, quarter, number):
        return a_all.at[rows(line, quarter), pl.ds(number * block, block)]

    def arrived(ref, sem):
        pltpu.make_async_copy(ref, ref, sem).wait()

    def role(zz):
        inner = zz in (1, 2)
        mate = {0: 1, 1: 2, 2: 1, 3: 2}[zz]

        def g_wait(line, quarter, piece):
            arrived(g_piece(line, quarter, piece), g_recv.at[line, quarter, piece])

        def g_forward(line, quarter, piece, target, send):
            ref = g_piece(line, quarter, piece)
            remote(ref, ref, send, g_recv.at[line, quarter, piece], target, s).start()

        def a_wait(line, quarter, number):
            arrived(a_piece(line, quarter, number), a_recv.at[line, quarter, number])

        def a_forward(line, quarter, number, target, target_quarter, send):
            ref = a_piece(line, quarter, number)
            remote(ref, ref, send, a_recv.at[line, quarter, number], target, target_quarter).start()

        def spread(line):
            for number in NEED[zz]:
                for quarter in (core_peer, y_peer):
                    a_forward(line, s, number, zz, quarter, act_row)

        def relay(line):
            for number in NEED[zz]:
                a_wait(line, y_peer, number)
                a_forward(line, y_peer, number, zz, core_peer, act_row)

        for place, quarter in enumerate(peers):
            for piece in (0, 1):
                start = quarter * width + piece * near
                size = far if piece else near
                source = grads.at[:, pl.ds(pl.multiple_of(start, 128), size)]
                target = g_piece(zz, s, piece)
                sem = g_recv.at[zz, s, piece]
                if piece and not inner:
                    remote(source, target, row_send, sem, mate, quarter).start()
                elif place == 0:
                    pltpu.make_async_copy(source, target, sem).start()
                else:
                    remote(source, target, row_send, sem, zz, quarter).start()
        for number in NEED[zz]:
            own = act.at[:, pl.ds(number * block, block)]
            pltpu.make_async_copy(own, a_piece(zz, s, number), a_recv.at[zz, s, number]).start()
        for target, numbers, send in (
            (zz + 1, RIGHTWARD.get(zz + 1, ()), act_right), (zz - 1, LEFTWARD.get(zz - 1, ()), act_left),
        ):
            for number in numbers:
                own = act.at[:, pl.ds(number * block, block)]
                sem = a_recv.at[zz, s, number]
                remote(own, a_piece(zz, s, number), send, sem, target, s).start()

        for quarter in peers:
            g_wait(zz, quarter, 0)
            if zz < LINE - 1:
                g_forward(zz, quarter, 0, zz + 1, right_a)
            if zz > 0:
                g_forward(zz, quarter, 0, zz - 1, left_a)
            if inner:
                g_wait(zz, quarter, 1)
                g_forward(zz, quarter, 1, mate, right_b if zz == 1 else left_b)

        for place, quarter in enumerate(peers):
            start = pl.multiple_of(quarter * width, 128)
            held = pl.ds(pl.multiple_of(s * q_rows, q_rows), q_rows)
            size = width if inner else near
            source = query.at[:, pl.ds(start, size)]
            target = q_own.at[held, pl.ds(0, size)]
            if place == 0:
                pltpu.make_async_copy(source, target, q_recv.at[s]).start()
            else:
                remote(source, target, q_send, q_recv.at[s], zz, quarter).start()
            if not inner:
                source = query.at[:, pl.ds(pl.multiple_of(start + near, 128), far)]
                remote(source, q_next.at[held, :], q_send, n_recv.at[s], mate, quarter).start()
        for number in NEED[zz]:
            a_wait(zz, s, number)
        spread(zz)

        for distance in range(1, LINE):
            from_left, from_right = zz - distance, zz + distance
            if from_left >= 0:
                for number in RIGHTWARD[zz]:
                    a_wait(from_left, s, number)
                for number in RIGHTWARD.get(zz + 1, ()):
                    a_forward(from_left, s, number, zz + 1, s, act_right)
                spread(from_left)
            if from_right < LINE:
                for number in LEFTWARD[zz]:
                    a_wait(from_right, s, number)
                for number in LEFTWARD.get(zz - 1, ()):
                    a_forward(from_right, s, number, zz - 1, s, act_left)
                spread(from_right)
            for quarter in peers:
                if from_left >= 0:
                    g_wait(from_left, quarter, 0)
                    if zz < LINE - 1:
                        g_forward(from_left, quarter, 0, zz + 1, right_a)
                if from_right < LINE:
                    g_wait(from_right, quarter, 0)
                    if zz > 0:
                        g_forward(from_right, quarter, 0, zz - 1, left_a)
                if inner and from_left >= 0:
                    g_wait(from_left, quarter, 1)
                    if zz == 1:
                        g_forward(from_left, quarter, 1, mate, right_b)
                if inner and from_right < LINE:
                    g_wait(from_right, quarter, 1)
                    if zz == 2:
                        g_forward(from_right, quarter, 1, mate, left_b)
            if distance == 1:
                relay(zz)
            if from_left >= 0:
                relay(from_left)
            if from_right < LINE:
                relay(from_right)

        for line in range(LINE):
            for quarter in (core_peer, diagonal):
                for number in NEED[zz]:
                    a_wait(line, quarter, number)
        for quarter in range(ROW):
            held = pl.ds(quarter * q_rows, q_rows)
            size = width if inner else near
            arrived(q_own.at[held, pl.ds(0, size)], q_recv.at[quarter])
            if inner:
                arrived(q_next.at[held, :], n_recv.at[quarter])

        sent = 3 * width if inner else 3 * width + far
        arrived(grads.at[:, pl.ds(0, sent)], row_send)
        arrived(query.at[:, pl.ds(0, sent)], q_send)
        line_rows = ROW * tokens
        if zz < LINE - 1:
            arrived(g_all.at[pl.ds(0, (zz + 1) * line_rows), pl.ds(0, near)], right_a)
            wide = len(RIGHTWARD[zz + 1]) * block
            arrived(a_all.at[pl.ds(0, (zz + 1) * tokens), pl.ds(0, wide)], act_right)
        if zz > 0:
            arrived(g_all.at[pl.ds(0, (LINE - zz) * line_rows), pl.ds(0, near)], left_a)
            wide = len(LEFTWARD[zz - 1]) * block
            arrived(a_all.at[pl.ds(0, (LINE - zz) * tokens), pl.ds(0, wide)], act_left)
        if inner:
            half = g_all.at[pl.ds(0, 2 * line_rows), pl.ds(near, far)]
            arrived(half, right_b if zz == 1 else left_b)
        wide = len(NEED[zz]) * block
        arrived(a_all.at[pl.ds(0, 3 * LINE * tokens), pl.ds(0, wide)], act_row)

    for zz in range(LINE):
        pl.when(z == zz)(functools.partial(role, zz))


def on_line(activations, out_grads, query_grad, token_order, doc_ids):
    tokens, features = activations.shape
    columns = out_grads.shape[1]
    width = columns // ROW
    near = width * 4 // 7 // 256 * 256
    far = width - near
    q_rows = query_grad.shape[0]
    count = ROW * LINE
    block = features // LINE
    position = lax.axis_index("tok")
    dma = pltpu.SemaphoreType.DMA
    g_all, a_all, q_own, q_next = pl.pallas_call(
        functools.partial(exchange, near),
        out_shape=(
            jax.ShapeDtypeStruct((count * tokens, width), jnp.bfloat16),
            jax.ShapeDtypeStruct((count * tokens, features), jnp.bfloat16),
            jax.ShapeDtypeStruct((ROW * q_rows, width), jnp.bfloat16),
            jax.ShapeDtypeStruct((ROW * q_rows, far), jnp.bfloat16),
        ),
        in_specs=[pl.BlockSpec(memory_space=pl.ANY)] * 3,
        out_specs=[pl.BlockSpec(memory_space=pl.ANY)] * 4,
        scratch_shapes=[
            dma((LINE, ROW, 2)), dma((LINE, ROW, LINE)), dma((ROW,)), dma((ROW,)),
        ] + [dma] * 9,
        compiler_params=pltpu.CompilerParams(collective_id=0, has_side_effects=True),
        name="exchange",
    )(activations, out_grads, query_grad)

    def end_scores(number):
        rows_in = a_all[:, number * block : (number + 1) * block]
        projected = jnp.dot(rows_in, q_own[:, :near], preferred_element_type=jnp.float32)
        return jnp.sum(projected * g_all[:, :near].astype(jnp.float32), axis=1)

    def inner_scores(number, mate):
        rows_in = a_all[:, number * block : (number + 1) * block]
        rows_mate = a_all[:, mate * block : (mate + 1) * block]
        extra = jnp.dot(rows_in, q_own[:, near:], preferred_element_type=jnp.float32)
        extra = extra + jnp.dot(rows_mate, q_next, preferred_element_type=jnp.float32)
        extra = jnp.sum(extra * g_all[:, near:].astype(jnp.float32), axis=1)
        return end_scores(number) + extra

    partial_value = lax.switch(
        position // ROW,
        [
            functools.partial(end_scores, 0),
            functools.partial(inner_scores, 1, 0),
            functools.partial(inner_scores, 2, 3),
            functools.partial(end_scores, 3),
        ],
    )
    example_of = jnp.take(doc_ids, token_order)
    example_count = E_DEV * count
    onehot = (example_of[:, None] == jnp.arange(example_count, dtype=jnp.int32)[None, :]).astype(
        jnp.float32
    )
    example_sums = jnp.dot(partial_value, onehot, precision=lax.Precision.HIGHEST)
    return lax.psum_scatter(example_sums, "tok", scatter_dimension=0, tiled=True)


def from_partner(array, axis, bit):
    return lax.ppermute(array, axis, [(i, i ^ 1 << bit) for i in range(lax.axis_size(axis))])


def shifted(value, axis, steps):
    count = lax.axis_size(axis)
    pairs = [(source, (source + steps) % count) for source in range(count)]
    return lax.ppermute(value, axis, pairs)


def order_rows(own_rows, other_rows, own_bit):
    lower_half = jnp.where(own_bit == 0, own_rows, other_rows)
    higher = jnp.where(own_bit == 0, other_rows, own_rows)
    return jnp.concatenate([lower_half, higher], axis=0)


def halve_columns(members, lower_bits, position):
    for bit_number in range(lower_bits):
        own_bit = position >> bit_number & 1
        retained = []
        outgoing = []
        for member in members:
            half_width = member.shape[1] // 2
            retained.append(lax.dynamic_slice_in_dim(member, own_bit * half_width, half_width, 1))
            outgoing.append(
                lax.dynamic_slice_in_dim(member, (1 - own_bit) * half_width, half_width, 1)
            )
        arrived = from_partner((outgoing[0], outgoing[1]), "tok", bit_number)
        members = (
            order_rows(retained[0], arrived[0], own_bit),
            order_rows(retained[1], arrived[1], own_bit),
        )
    return members


def double_rows(activations, lower_bits, position):
    for bit_number in range(lower_bits):
        own_bit = position >> bit_number & 1
        arrived = from_partner(activations, "tok", bit_number)
        activations = order_rows(activations, arrived, own_bit)
    return activations


def per_device(activations, out_grads, query_grad, token_order, doc_ids):
    axis_devices = lax.axis_size("tok")
    position = lax.axis_index("tok")
    lower_bits = 3
    window_size = 2**lower_bits
    group_count = axis_devices // window_size
    own_group = position // window_size
    query_rows, grad_rows = halve_columns((query_grad, out_grads), lower_bits, position)
    shared = double_rows(activations, lower_bits, position)
    block_rows = query_rows.shape[0]

    def accumulate(running, query_piece, first_group):
        row_start = first_group * block_rows
        columns = lax.dynamic_slice_in_dim(shared, row_start, query_piece.shape[0], 1)
        return running + jnp.dot(columns, query_piece, preferred_element_type=jnp.float32)

    running = accumulate(
        jnp.zeros((shared.shape[0], query_rows.shape[1]), jnp.float32), query_rows, own_group
    )

    def turn_single(turn_index, carried):
        partial_sum, query_piece = carried
        query_piece = shifted(query_piece, "tok", window_size)
        source = (own_group - turn_index - 1) % group_count
        return (accumulate(partial_sum, query_piece, source), query_piece)

    running, unused_piece = lax.fori_loop(0, group_count - 1, turn_single, (running, query_rows))
    partial_value = jnp.sum(running * grad_rows.astype(jnp.float32), axis=1)
    window_tokens = shared.shape[0]
    stored_order = lax.dynamic_slice_in_dim(
        token_order, own_group * window_tokens, window_tokens, 0
    )
    example_of = jnp.take(doc_ids, stored_order)
    example_count = E_DEV * axis_devices
    onehot = (example_of[:, None] == jnp.arange(example_count, dtype=jnp.int32)[None, :]).astype(
        jnp.float32
    )
    example_sums = jnp.dot(partial_value, onehot, precision=lax.Precision.HIGHEST)
    return lax.psum_scatter(example_sums, "tok", scatter_dimension=0, tiled=True)


def solution(mesh):
    placed = (
        P(("groups", "tok"), None),
        P(("groups", "tok"), None),
        P(("groups", "tok"), None),
        P("groups"),
        P("groups"),
    )
    local = on_line if mesh.shape["tok"] == ROW * LINE else per_device
    return jax.shard_map(
        local, mesh=mesh, in_specs=placed, out_specs=P(("groups", "tok")), check_vma=False
    )
```

```python
import functools

import jax
import jax.numpy as jnp
from jax import lax
from jax.experimental import pallas as pl
from jax.experimental.pallas import tpu as pltpu
from jax.sharding import PartitionSpec as P

E_DEV = 2
ROW = 4
LINE = 4
MESH = pl.DeviceIdType.MESH
NEED = ((0,), (0, 1), (2, 3), (3,))
RIGHTWARD = {1: (0, 1, 2, 3), 2: (2, 3), 3: (3,)}
LEFTWARD = {2: (0, 1, 2, 3), 1: (0, 1), 0: (0,)}


def exchange(
    near, act, grads, query, member, out, g_all, a_all, q_own, q_next, total, mine, slots,
    g_recv, a_recv, q_recv, n_recv, row_send, right_a, right_b, left_a, left_b, act_right, act_left,
    act_row, q_send, n_send,
    sum_recv, sum_send,
):
    me = lax.axis_index("tok")
    z = me // ROW
    s = me % ROW
    y, c = s // 2, s % 2
    tokens, features = act.shape
    q_rows = query.shape[0]
    width = g_all.shape[1]
    far = width - near
    block = features // LINE
    core_peer = y * 2 + 1 - c
    y_peer = (1 - y) * 2 + c
    diagonal = (1 - y) * 2 + 1 - c
    peers = (s, core_peer, y_peer, diagonal)

    barrier = pltpu.get_barrier_semaphore()
    for step in range(1, ROW * LINE):
        other = (me + step) % (ROW * LINE)
        pl.semaphore_signal(barrier, inc=1, device_id={"tok": other}, device_id_type=MESH)
    pl.semaphore_wait(barrier, ROW * LINE - 1)

    def remote(source, target, send, recv, line, quarter):
        return pltpu.make_async_remote_copy(
            src_ref=source, dst_ref=target, send_sem=send, recv_sem=recv,
            device_id={"tok": line * ROW + quarter}, device_id_type=MESH,
        )

    def rows(line, quarter):
        return pl.ds(pl.multiple_of((line * ROW + quarter) * tokens, tokens), tokens)

    def g_piece(line, quarter, piece):
        columns = pl.ds(0, near) if piece == 0 else pl.ds(near, far)
        return g_all.at[rows(line, quarter), columns]

    def a_piece(line, quarter, number):
        return a_all.at[rows(line, quarter), pl.ds(number * block, block)]

    def arrived(ref, sem):
        pltpu.make_async_copy(ref, ref, sem).wait()

    def role(zz, part):
        inner = zz in (1, 2)
        mate = {0: 1, 1: 2, 2: 1, 3: 2}[zz]

        def g_wait(line, quarter, piece):
            arrived(g_piece(line, quarter, piece), g_recv.at[line, quarter, piece])

        def g_forward(line, quarter, piece, target, send):
            ref = g_piece(line, quarter, piece)
            remote(ref, ref, send, g_recv.at[line, quarter, piece], target, s).start()

        def a_wait(line, quarter, number):
            arrived(a_piece(line, quarter, number), a_recv.at[line, quarter, number])

        def a_forward(line, quarter, number, target, target_quarter, send):
            ref = a_piece(line, quarter, number)
            remote(ref, ref, send, a_recv.at[line, quarter, number], target, target_quarter).start()

        def q_take(quarter):
            held = pl.ds(pl.multiple_of(quarter * q_rows, q_rows), q_rows)
            arrived(q_own.at[held, :], q_recv.at[quarter])
            if not inner:
                source = q_own.at[held, pl.ds(near, far)]
                remote(source, q_next.at[held, :], n_send, n_recv.at[quarter], mate, s).start()

        def spread(line):
            for number in NEED[zz]:
                for quarter in (core_peer, y_peer):
                    a_forward(line, s, number, zz, quarter, act_row)

        def relay(line):
            for number in NEED[zz]:
                a_wait(line, y_peer, number)
                a_forward(line, y_peer, number, zz, core_peer, act_row)

        def first(zz):
            for place, quarter in enumerate(peers):
                for piece in (0, 1):
                    start = quarter * width + piece * near
                    size = far if piece else near
                    source = grads.at[:, pl.ds(pl.multiple_of(start, 128), size)]
                    target = g_piece(zz, s, piece)
                    sem = g_recv.at[zz, s, piece]
                    if place == 0:
                        pltpu.make_async_copy(source, target, sem).start()
                    else:
                        remote(source, target, row_send, sem, zz, quarter).start()
            for number in NEED[zz]:
                own = act.at[:, pl.ds(number * block, block)]
                pltpu.make_async_copy(own, a_piece(zz, s, number), a_recv.at[zz, s, number]).start()
            for target, numbers, send in (
                (zz + 1, RIGHTWARD.get(zz + 1, ()), act_right), (zz - 1, LEFTWARD.get(zz - 1, ()), act_left),
            ):
                for number in numbers:
                    own = act.at[:, pl.ds(number * block, block)]
                    sem = a_recv.at[zz, s, number]
                    remote(own, a_piece(zz, s, number), send, sem, target, s).start()

            for quarter in peers:
                g_wait(zz, quarter, 0)
                if zz < LINE - 1:
                    g_forward(zz, quarter, 0, zz + 1, right_a)
                if zz > 0:
                    g_forward(zz, quarter, 0, zz - 1, left_a)
                g_wait(zz, quarter, 1)
                g_forward(zz, quarter, 1, mate, right_b if zz < 2 else left_b)

            for place, quarter in enumerate(peers):
                start = pl.multiple_of(quarter * width, 128)
                held = pl.ds(pl.multiple_of(s * q_rows, q_rows), q_rows)
                source = query.at[:, pl.ds(start, width)]
                target = q_own.at[held, :]
                if place == 0:
                    pltpu.make_async_copy(source, target, q_recv.at[s]).start()
                else:
                    remote(source, target, q_send, q_recv.at[s], zz, quarter).start()
            for number in NEED[zz]:
                a_wait(zz, s, number)
            spread(zz)
            for quarter in (s, core_peer):
                q_take(quarter)

        def drain(zz):
            arrived(grads.at[:, pl.ds(0, 3 * width)], row_send)
            arrived(query.at[:, pl.ds(0, 3 * width)], q_send)
            line_rows = ROW * tokens
            if zz < LINE - 1:
                arrived(g_all.at[pl.ds(0, (zz + 1) * line_rows), pl.ds(0, near)], right_a)
                wide = len(RIGHTWARD[zz + 1]) * block
                arrived(a_all.at[pl.ds(0, (zz + 1) * tokens), pl.ds(0, wide)], act_right)
            if zz > 0:
                arrived(g_all.at[pl.ds(0, (LINE - zz) * line_rows), pl.ds(0, near)], left_a)
                wide = len(LEFTWARD[zz - 1]) * block
                arrived(a_all.at[pl.ds(0, (LINE - zz) * tokens), pl.ds(0, wide)], act_left)
            half = g_all.at[pl.ds(0, (2 if inner else 1) * line_rows), pl.ds(near, far)]
            arrived(half, right_b if zz < 2 else left_b)
            if not inner:
                arrived(q_next, n_send)
            wide = len(NEED[zz]) * block
            arrived(a_all.at[pl.ds(0, 3 * LINE * tokens), pl.ds(0, wide)], act_row)

        last_line = LINE - 1 if zz < 2 else 0
        last_distance = abs(last_line - zz)

        def acts_in(distance):
            from_left, from_right = zz - distance, zz + distance
            if from_left >= 0:
                for number in RIGHTWARD[zz]:
                    a_wait(from_left, s, number)
                for number in RIGHTWARD.get(zz + 1, ()):
                    a_forward(from_left, s, number, zz + 1, s, act_right)
                spread(from_left)
            if from_right < LINE:
                for number in LEFTWARD[zz]:
                    a_wait(from_right, s, number)
                for number in LEFTWARD.get(zz - 1, ()):
                    a_forward(from_right, s, number, zz - 1, s, act_left)
                spread(from_right)

        def grads_in(distance, quarter):
            from_left, from_right = zz - distance, zz + distance
            if from_left >= 0:
                g_wait(from_left, quarter, 0)
                if zz < LINE - 1:
                    g_forward(from_left, quarter, 0, zz + 1, right_a)
            if from_right < LINE:
                g_wait(from_right, quarter, 0)
                if zz > 0:
                    g_forward(from_right, quarter, 0, zz - 1, left_a)
            if inner and from_left >= 0:
                g_wait(from_left, quarter, 1)
                if zz == 1:
                    g_forward(from_left, quarter, 1, mate, right_b)
            if inner and from_right < LINE:
                g_wait(from_right, quarter, 1)
                if zz == 2:
                    g_forward(from_right, quarter, 1, mate, left_b)

        def acts_ready(line):
            for quarter in (core_peer, diagonal):
                for number in NEED[zz]:
                    a_wait(line, quarter, number)

        if part == 0:
            first(zz)
            for distance in range(1, last_distance):
                acts_in(distance)
                for quarter in peers:
                    grads_in(distance, quarter)
                if distance == 1:
                    for quarter in (y_peer, diagonal):
                        q_take(quarter)
                    relay(zz)
                for line in (zz - distance, zz + distance):
                    if 0 <= line < LINE:
                        relay(line)
            acts_in(last_distance)
            for quarter in peers[:2]:
                grads_in(last_distance, quarter)
            for line in range(LINE):
                if line != last_line:
                    acts_ready(line)
        elif part == 1:
            grads_in(last_distance, peers[2])
            relay(last_line)
            if inner:
                for quarter in range(ROW):
                    held = pl.ds(quarter * q_rows, q_rows)
                    arrived(q_next.at[held, :], n_recv.at[quarter])
        elif part == 2:
            grads_in(last_distance, peers[3])
            acts_ready(last_line)
        else:
            drain(zz)

    def run(part):
        for zz in range(LINE):
            pl.when(z == zz)(functools.partial(role, zz, part))

    tall = 2 * tokens
    tile = 512
    is_inner = (z == 1) | (z == 2)
    first_rows = pl.multiple_of((z // 2) * ROW * tokens, tokens)
    last_rows = pl.multiple_of((1 - z // 2) * (LINE - 1) * ROW * tokens, tokens)
    near_act = pl.ds(pl.multiple_of(z * block, block), block)
    mate_line = z + 1 - 2 * (z % 2)
    mate_act = pl.ds(pl.multiple_of(mate_line * block, block), block)

    def add(held, projected, columns):
        weighed = projected * g_all[held, columns].astype(jnp.float32)
        parts = [weighed[:, i * 128 : (i + 1) * 128] for i in range(tile // 128)]
        total[held, :] += sum(parts[1:], parts[0])

    def near_block(start, count):
        def step(number, carried):
            held = pl.ds(pl.multiple_of(start + number % count * tall, tall), tall)
            columns = pl.ds(pl.multiple_of(number // count * tile, tile), tile)
            add(held, jnp.dot(
                a_all[held, near_act], q_own[:, columns], preferred_element_type=jnp.float32
            ), columns)
            return carried

        lax.fori_loop(0, near // tile * count, step, 0)

    def far_block(start, count):
        def step(number, carried):
            held = pl.ds(pl.multiple_of(start + number % count * tall, tall), tall)
            local = pl.multiple_of(number // count * tile, tile)
            columns = pl.ds(pl.multiple_of(near + local, tile), tile)
            projected = jnp.dot(
                a_all[held, near_act], q_own[:, columns], preferred_element_type=jnp.float32
            ) + jnp.dot(
                a_all[held, mate_act], q_next[:, pl.ds(local, tile)],
                preferred_element_type=jnp.float32,
            )
            add(held, projected, columns)
            return carried

        @pl.when(is_inner)
        def _():
            lax.fori_loop(0, far // tile * count, step, 0)

    whole = (LINE - 1) * ROW // 2
    total[...] = jnp.zeros_like(total)
    run(0)
    near_block(first_rows, whole)
    run(1)
    far_block(first_rows, whole)
    early = pl.multiple_of(last_rows + y * tall, tall)
    late = pl.multiple_of(last_rows + (1 - y) * tall, tall)
    run(2)
    near_block(early, 1)
    far_block(early, 1)
    near_block(late, 1)
    far_block(late, 1)

    token_scores = jnp.sum(total[...], axis=1, keepdims=True)
    sums = jnp.sum(token_scores * member[...], axis=0, keepdims=True)
    mine[...] = jnp.broadcast_to(sums, mine.shape)
    slots[me] = mine[...]
    for step in range(1, ROW * LINE):
        other = (me + step) % (ROW * LINE)
        pltpu.make_async_remote_copy(
            src_ref=mine, dst_ref=slots.at[me], send_sem=sum_send, recv_sem=sum_recv.at[me],
            device_id={"tok": other}, device_id_type=MESH,
        ).start()
    for step in range(1, ROW * LINE):
        other = (me + step) % (ROW * LINE)
        arrived(slots.at[other], sum_recv.at[other])
    out[...] = jnp.sum(slots[...], axis=0)
    arrived(slots.at[pl.ds(0, ROW * LINE - 1)], sum_send)
    run(3)


def on_line(activations, out_grads, query_grad, token_order, doc_ids):
    tokens, features = activations.shape
    columns = out_grads.shape[1]
    width = columns // ROW
    near = width * 4 // 7 // 256 * 256
    far = width - near
    q_rows = query_grad.shape[0]
    count = ROW * LINE
    position = lax.axis_index("tok")
    dma = pltpu.SemaphoreType.DMA
    examples = E_DEV * count
    places = jnp.arange(examples, dtype=jnp.int32)
    begin = jnp.sum((doc_ids[:, None] < places[None, :]).astype(jnp.int32), axis=0)
    end = jnp.sum((doc_ids[:, None] <= places[None, :]).astype(jnp.int32), axis=0)
    member = (token_order[:, None] >= begin[None, :]) & (token_order[:, None] < end[None, :])
    member = jnp.pad(member.astype(jnp.float32), ((0, 0), (0, 128 - examples)))
    vmem = pltpu.VMEM
    sums = pl.pallas_call(
        functools.partial(exchange, near),
        out_shape=jax.ShapeDtypeStruct((8, 128), jnp.float32),
        in_specs=[pl.BlockSpec(memory_space=pl.ANY)] * 3 + [pl.BlockSpec(memory_space=vmem)],
        out_specs=pl.BlockSpec(memory_space=vmem),
        scratch_shapes=[
            vmem((count * tokens, width), jnp.bfloat16),
            vmem((count * tokens, features), jnp.bfloat16),
            vmem((ROW * q_rows, width), jnp.bfloat16),
            vmem((ROW * q_rows, far), jnp.bfloat16),
            vmem((count * tokens, 128), jnp.float32),
            vmem((8, 128), jnp.float32),
            vmem((count, 8, 128), jnp.float32),
            dma((LINE, ROW, 2)), dma((LINE, ROW, LINE)), dma((ROW,)), dma((ROW,)),
        ] + [dma] * 10 + [dma((count,)), dma],
        compiler_params=pltpu.CompilerParams(
            collective_id=0, has_side_effects=True, vmem_limit_bytes=56 * 2**20
        ),
        name="exchange",
    )(activations, out_grads, query_grad, member)
    return lax.dynamic_slice(sums[0], (E_DEV * position,), (E_DEV,))


def from_partner(array, axis, bit):
    return lax.ppermute(array, axis, [(i, i ^ 1 << bit) for i in range(lax.axis_size(axis))])


def shifted(value, axis, steps):
    count = lax.axis_size(axis)
    pairs = [(source, (source + steps) % count) for source in range(count)]
    return lax.ppermute(value, axis, pairs)


def order_rows(own_rows, other_rows, own_bit):
    lower_half = jnp.where(own_bit == 0, own_rows, other_rows)
    higher = jnp.where(own_bit == 0, other_rows, own_rows)
    return jnp.concatenate([lower_half, higher], axis=0)


def halve_columns(members, lower_bits, position):
    for bit_number in range(lower_bits):
        own_bit = position >> bit_number & 1
        retained = []
        outgoing = []
        for member in members:
            half_width = member.shape[1] // 2
            retained.append(lax.dynamic_slice_in_dim(member, own_bit * half_width, half_width, 1))
            outgoing.append(
                lax.dynamic_slice_in_dim(member, (1 - own_bit) * half_width, half_width, 1)
            )
        arrived = from_partner((outgoing[0], outgoing[1]), "tok", bit_number)
        members = (
            order_rows(retained[0], arrived[0], own_bit),
            order_rows(retained[1], arrived[1], own_bit),
        )
    return members


def double_rows(activations, lower_bits, position):
    for bit_number in range(lower_bits):
        own_bit = position >> bit_number & 1
        arrived = from_partner(activations, "tok", bit_number)
        activations = order_rows(activations, arrived, own_bit)
    return activations


def per_device(activations, out_grads, query_grad, token_order, doc_ids):
    axis_devices = lax.axis_size("tok")
    position = lax.axis_index("tok")
    lower_bits = 3
    window_size = 2**lower_bits
    group_count = axis_devices // window_size
    own_group = position // window_size
    query_rows, grad_rows = halve_columns((query_grad, out_grads), lower_bits, position)
    shared = double_rows(activations, lower_bits, position)
    block_rows = query_rows.shape[0]

    def accumulate(running, query_piece, first_group):
        row_start = first_group * block_rows
        columns = lax.dynamic_slice_in_dim(shared, row_start, query_piece.shape[0], 1)
        return running + jnp.dot(columns, query_piece, preferred_element_type=jnp.float32)

    running = accumulate(
        jnp.zeros((shared.shape[0], query_rows.shape[1]), jnp.float32), query_rows, own_group
    )

    def turn_single(turn_index, carried):
        partial_sum, query_piece = carried
        query_piece = shifted(query_piece, "tok", window_size)
        source = (own_group - turn_index - 1) % group_count
        return (accumulate(partial_sum, query_piece, source), query_piece)

    running, unused_piece = lax.fori_loop(0, group_count - 1, turn_single, (running, query_rows))
    partial_value = jnp.sum(running * grad_rows.astype(jnp.float32), axis=1)
    window_tokens = shared.shape[0]
    stored_order = lax.dynamic_slice_in_dim(
        token_order, own_group * window_tokens, window_tokens, 0
    )
    example_of = jnp.take(doc_ids, stored_order)
    example_count = E_DEV * axis_devices
    onehot = (example_of[:, None] == jnp.arange(example_count, dtype=jnp.int32)[None, :]).astype(
        jnp.float32
    )
    example_sums = jnp.dot(partial_value, onehot, precision=lax.Precision.HIGHEST)
    return lax.psum_scatter(example_sums, "tok", scatter_dimension=0, tiled=True)


def solution(mesh):
    placed = (
        P(("groups", "tok"), None),
        P(("groups", "tok"), None),
        P(("groups", "tok"), None),
        P("groups"),
        P("groups"),
    )
    local = on_line if mesh.shape["tok"] == ROW * LINE else per_device
    return jax.shard_map(
        local, mesh=mesh, in_specs=placed, out_specs=P(("groups", "tok")), check_vma=False
    )
```

```python
import functools

import jax
import jax.numpy as jnp
from jax import lax
from jax.experimental import pallas as pl
from jax.experimental.pallas import tpu as pltpu
from jax.sharding import PartitionSpec as P

E_DEV = 2
ROW = 4
LINE = 4
MESH = pl.DeviceIdType.MESH
SPAN = (1, 2, 2, 1)
NEED = ((0,), (0,), (2,), (3,))
RIGHTWARD = {1: (0, 2), 2: (2,), 3: (3,)}
LEFTWARD = {2: (0, 2), 1: (0,), 0: (0,)}


def exchange(
    near, act, grads, query, order, docs, out, g_all, a_all, q_own, q_next, total, mine, slots, final,
    g_recv, a_recv, q_recv, n_recv, row_send, right_a, right_b, left_a, left_b, act_right, act_left,
    act_row, q_send, n_send,
    sum_recv, sum_send,
):
    me = lax.axis_index("tok")
    z = me // ROW
    s = me % ROW
    y, c = s // 2, s % 2
    tokens, features = act.shape
    q_rows = query.shape[0]
    width = g_all.shape[1]
    far = width - near
    block = features // LINE
    core_peer = y * 2 + 1 - c
    y_peer = (1 - y) * 2 + c
    diagonal = (1 - y) * 2 + 1 - c
    peers = (s, core_peer, y_peer, diagonal)

    barrier = pltpu.get_barrier_semaphore()
    for step in range(1, ROW * LINE):
        other = (me + step) % (ROW * LINE)
        pl.semaphore_signal(barrier, inc=1, device_id={"tok": other}, device_id_type=MESH)
    pl.semaphore_wait(barrier, ROW * LINE - 1)

    def remote(source, target, send, recv, line, quarter):
        return pltpu.make_async_remote_copy(
            src_ref=source, dst_ref=target, send_sem=send, recv_sem=recv,
            device_id={"tok": line * ROW + quarter}, device_id_type=MESH,
        )

    def rows(line, quarter):
        return pl.ds(pl.multiple_of((line * ROW + quarter) * tokens, tokens), tokens)

    def g_piece(line, quarter, piece):
        columns = pl.ds(0, near) if piece == 0 else pl.ds(near, far)
        return g_all.at[rows(line, quarter), columns]

    def a_piece(line, quarter, number, target):
        return a_all.at[rows(line, quarter), pl.ds(number * block, SPAN[target] * block)]

    def arrived(ref, sem):
        pltpu.make_async_copy(ref, ref, sem).wait()

    def role(zz, part):
        inner = zz in (1, 2)
        mate = {0: 1, 1: 2, 2: 1, 3: 2}[zz]

        def g_wait(line, quarter, piece):
            arrived(g_piece(line, quarter, piece), g_recv.at[line, quarter, piece])

        def g_forward(line, quarter, piece, target, send):
            ref = g_piece(line, quarter, piece)
            remote(ref, ref, send, g_recv.at[line, quarter, piece], target, s).start()

        def a_wait(line, quarter, number):
            arrived(a_piece(line, quarter, number, zz), a_recv.at[line, quarter, number])

        def a_forward(line, quarter, number, target, target_quarter, send):
            ref = a_piece(line, quarter, number, target)
            remote(ref, ref, send, a_recv.at[line, quarter, number], target, target_quarter).start()

        def q_piece(quarter, piece):
            held = pl.ds(pl.multiple_of(quarter * q_rows, q_rows), q_rows)
            return q_own.at[held, pl.ds(0, near) if piece == 0 else pl.ds(near, far)]

        def q_give(places, piece):
            for place in places:
                quarter = peers[place]
                start = pl.multiple_of(quarter * width + piece * near, 128)
                source = query.at[:, pl.ds(start, far if piece else near)]
                sem = q_recv.at[s, piece]
                if place == 0:
                    pltpu.make_async_copy(source, q_piece(s, piece), sem).start()
                else:
                    remote(source, q_piece(s, piece), q_send, sem, zz, quarter).start()

        def q_take(places, piece):
            for place in places:
                quarter = peers[place]
                arrived(q_piece(quarter, piece), q_recv.at[quarter, piece])
                if piece and not inner:
                    held = pl.ds(pl.multiple_of(quarter * q_rows, q_rows), q_rows)
                    remote(
                        q_piece(quarter, 1), q_next.at[held, :], n_send, n_recv.at[quarter], mate, s
                    ).start()

        def spread(line):
            for number in NEED[zz]:
                for quarter in (core_peer, y_peer):
                    a_forward(line, s, number, zz, quarter, act_row)

        def relay(line):
            for number in NEED[zz]:
                a_wait(line, y_peer, number)
                a_forward(line, y_peer, number, zz, core_peer, act_row)

        def first(zz):
            for place, quarter in enumerate(peers):
                for piece in (0, 1):
                    start = quarter * width + piece * near
                    size = far if piece else near
                    source = grads.at[:, pl.ds(pl.multiple_of(start, 128), size)]
                    target = g_piece(zz, s, piece)
                    sem = g_recv.at[zz, s, piece]
                    if place == 0:
                        pltpu.make_async_copy(source, target, sem).start()
                    else:
                        remote(source, target, row_send, sem, zz, quarter).start()
            for number in NEED[zz]:
                own = act.at[:, pl.ds(number * block, SPAN[zz] * block)]
                pltpu.make_async_copy(own, a_piece(zz, s, number, zz), a_recv.at[zz, s, number]).start()
            for target, numbers, send in (
                (zz + 1, RIGHTWARD.get(zz + 1, ()), act_right), (zz - 1, LEFTWARD.get(zz - 1, ()), act_left),
            ):
                for number in numbers:
                    own = act.at[:, pl.ds(number * block, SPAN[target] * block)]
                    sem = a_recv.at[zz, s, number]
                    remote(own, a_piece(zz, s, number, target), send, sem, target, s).start()

            for quarter in peers:
                g_wait(zz, quarter, 0)
                if zz < LINE - 1:
                    g_forward(zz, quarter, 0, zz + 1, right_a)
                if zz > 0:
                    g_forward(zz, quarter, 0, zz - 1, left_a)
                g_wait(zz, quarter, 1)
                g_forward(zz, quarter, 1, mate, right_b if zz < 2 else left_b)

            for number in NEED[zz]:
                a_wait(zz, s, number)
            spread(zz)

        def drain(zz):
            arrived(grads.at[:, pl.ds(0, 3 * width)], row_send)
            arrived(query.at[:, pl.ds(0, 3 * width)], q_send)
            line_rows = ROW * tokens
            if zz < LINE - 1:
                arrived(g_all.at[pl.ds(0, (zz + 1) * line_rows), pl.ds(0, near)], right_a)
                wide = len(RIGHTWARD[zz + 1]) * SPAN[zz + 1] * block
                arrived(a_all.at[pl.ds(0, (zz + 1) * tokens), pl.ds(0, wide)], act_right)
            if zz > 0:
                arrived(g_all.at[pl.ds(0, (LINE - zz) * line_rows), pl.ds(0, near)], left_a)
                wide = len(LEFTWARD[zz - 1]) * SPAN[zz - 1] * block
                arrived(a_all.at[pl.ds(0, (LINE - zz) * tokens), pl.ds(0, wide)], act_left)
            half = g_all.at[pl.ds(0, (2 if inner else 1) * line_rows), pl.ds(near, far)]
            arrived(half, right_b if zz < 2 else left_b)
            if not inner:
                arrived(q_next, n_send)
            wide = SPAN[zz] * block
            arrived(a_all.at[pl.ds(0, 3 * LINE * tokens), pl.ds(0, wide)], act_row)

        last_line = LINE - 1 if zz < 2 else 0
        outside = {1: 0, 2: 3}.get(zz, -1)

        def acts_in(distance):
            from_left, from_right = zz - distance, zz + distance
            if from_left >= 0:
                for number in RIGHTWARD[zz]:
                    a_wait(from_left, s, number)
                for number in RIGHTWARD.get(zz + 1, ()):
                    a_forward(from_left, s, number, zz + 1, s, act_right)
                spread(from_left)
            if from_right < LINE:
                for number in LEFTWARD[zz]:
                    a_wait(from_right, s, number)
                for number in LEFTWARD.get(zz - 1, ()):
                    a_forward(from_right, s, number, zz - 1, s, act_left)
                spread(from_right)

        def grads_in(line, piece):
            for quarter in peers:
                g_wait(line, quarter, piece)
                if piece == 0 and line < zz < LINE - 1:
                    g_forward(line, quarter, 0, zz + 1, right_a)
                if piece == 0 and line > zz > 0:
                    g_forward(line, quarter, 0, zz - 1, left_a)
                if piece == 1 and line == outside:
                    g_forward(line, quarter, 1, mate, right_b if zz == 1 else left_b)

        def acts_ready(line):
            for quarter in (core_peer, diagonal):
                for number in NEED[zz]:
                    a_wait(line, quarter, number)

        early_lines = [line for line in range(LINE) if line != last_line]
        if part == 0:
            first(zz)
            if inner:
                acts_in(1)
                q_give((1, 2, 3, 0), 0)
                q_give((1, 2, 3, 0), 1)
                grads_in(outside, 0)
                grads_in(mate, 0)
                acts_in(2)
                grads_in(outside, 1)
                grads_in(last_line, 0)
                relay(zz)
                relay(mate)
                relay(outside)
                relay(last_line)
                q_take((0, 1, 2, 3), 0)
            else:
                q_give((1, 2, 3, 0), 1)
                q_give((1, 0), 0)
                q_take((0, 1), 1)
                acts_in(1)
                q_take((2, 3), 1)
                q_give((2, 3), 0)
                relay(zz)
                grads_in(mate, 0)
                relay(mate)
                acts_in(2)
                grads_in(3 - mate, 0)
                relay(3 - mate)
                acts_in(3)
                q_take((0, 1, 2, 3), 0)
            for line in early_lines:
                acts_ready(line)
        elif part == 1:
            if not inner:
                grads_in(last_line, 0)
                relay(last_line)
            acts_ready(last_line)
        elif part == 2:
            if inner:
                q_take((0, 1, 2, 3), 1)
                grads_in(mate, 1)
                for quarter in range(ROW):
                    held = pl.ds(quarter * q_rows, q_rows)
                    arrived(q_next.at[held, :], n_recv.at[quarter])
        elif part == 3:
            if inner:
                for quarter in peers[:2]:
                    g_wait(last_line, quarter, 1)
        elif part == 4:
            if inner:
                for quarter in peers[2:]:
                    g_wait(last_line, quarter, 1)
        else:
            drain(zz)

    def run(part):
        for zz in range(LINE):
            pl.when(z == zz)(functools.partial(role, zz, part))

    tall = 2 * tokens
    tile = 512
    is_inner = (z == 1) | (z == 2)
    first_rows = pl.multiple_of((z // 2) * ROW * tokens, tokens)
    last_rows = pl.multiple_of((1 - z // 2) * (LINE - 1) * ROW * tokens, tokens)
    near_act = pl.ds(pl.multiple_of(z * block, block), block)
    mate_line = z + 1 - 2 * (z % 2)
    mate_act = pl.ds(pl.multiple_of(mate_line * block, block), block)

    def add(held, projected, columns):
        weighed = projected * g_all[held, columns].astype(jnp.float32)
        parts = [weighed[:, i * 128 : (i + 1) * 128] for i in range(tile // 128)]
        total[held, :] += sum(parts[1:], parts[0])

    def near_block(start, count):
        def step(number, carried):
            held = pl.ds(pl.multiple_of(start + number % count * tall, tall), tall)
            columns = pl.ds(pl.multiple_of(number // count * tile, tile), tile)
            add(held, jnp.dot(
                a_all[held, near_act], q_own[:, columns], preferred_element_type=jnp.float32
            ), columns)
            return carried

        lax.fori_loop(0, near // tile * count, step, 0)

    def far_block(start, count):
        def step(number, carried):
            held = pl.ds(pl.multiple_of(start + number % count * tall, tall), tall)
            local = pl.multiple_of(number // count * tile, tile)
            columns = pl.ds(pl.multiple_of(near + local, tile), tile)
            projected = jnp.dot(
                a_all[held, near_act], q_own[:, columns], preferred_element_type=jnp.float32
            ) + jnp.dot(
                a_all[held, mate_act], q_next[:, pl.ds(local, tile)],
                preferred_element_type=jnp.float32,
            )
            add(held, projected, columns)
            return carried

        @pl.when(is_inner)
        def _():
            lax.fori_loop(0, far // tile * count, step, 0)

    whole = (LINE - 1) * ROW // 2
    early = pl.multiple_of(last_rows + y * tall, tall)
    late = pl.multiple_of(last_rows + (1 - y) * tall, tall)
    run(0)
    total[...] = jnp.zeros_like(total)
    near_block(first_rows, whole)
    run(1)
    near_block(last_rows, 2)
    run(2)
    far_block(first_rows, whole)
    examples = mine.shape[0]
    numbers = lax.broadcasted_iota(jnp.int32, (examples, order.shape[1]), 0)
    begin = jnp.sum((docs[...] < numbers).astype(jnp.int32), axis=1, keepdims=True)
    end = jnp.sum((docs[...] <= numbers).astype(jnp.int32), axis=1, keepdims=True)

    def example_sums(start, size):
        held = pl.ds(start, size)
        scores = lax.dot_general(
            jnp.ones((8, 128), jnp.float32), total[held, :], (((1,), (1,)), ((), ())),
            precision=lax.Precision.HIGHEST, preferred_element_type=jnp.float32,
        )[0:1, :]
        place = order[:, held]
        member = (place >= begin) & (place < end)
        return jnp.sum(jnp.where(member, scores, 0.0), axis=1, keepdims=True)

    sums = example_sums(first_rows, whole * tall)
    run(3)
    far_block(early, 1)
    sums = sums + example_sums(early, tall)
    run(4)
    far_block(late, 1)
    sums = sums + example_sums(late, tall)

    mine[...] = jnp.broadcast_to(sums, mine.shape)
    slots[me] = mine[...]
    for step in range(1, ROW * LINE):
        other = (me + step) % (ROW * LINE)
        pltpu.make_async_remote_copy(
            src_ref=mine, dst_ref=slots.at[me], send_sem=sum_send, recv_sem=sum_recv.at[me],
            device_id={"tok": other}, device_id_type=MESH,
        ).start()
    for step in range(1, ROW * LINE):
        other = (me + step) % (ROW * LINE)
        arrived(slots.at[other], sum_recv.at[other])
    mine_sum = jnp.sum(slots[...], axis=0)
    final[...] = mine_sum
    out[...] = final[pl.ds(E_DEV * me, E_DEV), :]
    arrived(slots.at[pl.ds(0, ROW * LINE - 1)], sum_send)
    run(5)


def on_line(activations, out_grads, query_grad, token_order, doc_ids):
    tokens, features = activations.shape
    columns = out_grads.shape[1]
    width = columns // ROW
    near = width * 4 // 7 // 256 * 256
    far = width - near
    q_rows = query_grad.shape[0]
    count = ROW * LINE
    dma = pltpu.SemaphoreType.DMA
    examples = E_DEV * count
    vmem = pltpu.VMEM
    sums = pl.pallas_call(
        functools.partial(exchange, near),
        out_shape=jax.ShapeDtypeStruct((E_DEV, 128), jnp.float32),
        in_specs=[pl.BlockSpec(memory_space=pl.ANY)] * 3 + [pl.BlockSpec(memory_space=vmem)] * 2,
        out_specs=pl.BlockSpec(memory_space=vmem),
        scratch_shapes=[
            vmem((count * tokens, width), jnp.bfloat16),
            vmem((count * tokens, features), jnp.bfloat16),
            vmem((ROW * q_rows, width), jnp.bfloat16),
            vmem((ROW * q_rows, far), jnp.bfloat16),
            vmem((count * tokens, 128), jnp.float32),
            vmem((examples, 128), jnp.float32),
            vmem((count, examples, 128), jnp.float32),
            vmem((examples, 128), jnp.float32),
            dma((LINE, ROW, 2)), dma((LINE, ROW, LINE)), dma((ROW, 2)), dma((ROW,)),
        ] + [dma] * 10 + [dma((count,)), dma],
        compiler_params=pltpu.CompilerParams(
            collective_id=0, has_side_effects=True, vmem_limit_bytes=56 * 2**20
        ),
        name="exchange",
    )(
        activations, out_grads, query_grad, token_order.reshape(1, -1), doc_ids.reshape(1, -1)
    )
    return sums[:, 0]


def from_partner(array, axis, bit):
    return lax.ppermute(array, axis, [(i, i ^ 1 << bit) for i in range(lax.axis_size(axis))])


def shifted(value, axis, steps):
    count = lax.axis_size(axis)
    pairs = [(source, (source + steps) % count) for source in range(count)]
    return lax.ppermute(value, axis, pairs)


def order_rows(own_rows, other_rows, own_bit):
    lower_half = jnp.where(own_bit == 0, own_rows, other_rows)
    higher = jnp.where(own_bit == 0, other_rows, own_rows)
    return jnp.concatenate([lower_half, higher], axis=0)


def halve_columns(members, lower_bits, position):
    for bit_number in range(lower_bits):
        own_bit = position >> bit_number & 1
        retained = []
        outgoing = []
        for member in members:
            half_width = member.shape[1] // 2
            retained.append(lax.dynamic_slice_in_dim(member, own_bit * half_width, half_width, 1))
            outgoing.append(
                lax.dynamic_slice_in_dim(member, (1 - own_bit) * half_width, half_width, 1)
            )
        arrived = from_partner((outgoing[0], outgoing[1]), "tok", bit_number)
        members = (
            order_rows(retained[0], arrived[0], own_bit),
            order_rows(retained[1], arrived[1], own_bit),
        )
    return members


def double_rows(activations, lower_bits, position):
    for bit_number in range(lower_bits):
        own_bit = position >> bit_number & 1
        arrived = from_partner(activations, "tok", bit_number)
        activations = order_rows(activations, arrived, own_bit)
    return activations


def per_device(activations, out_grads, query_grad, token_order, doc_ids):
    axis_devices = lax.axis_size("tok")
    position = lax.axis_index("tok")
    lower_bits = 3
    window_size = 2**lower_bits
    group_count = axis_devices // window_size
    own_group = position // window_size
    query_rows, grad_rows = halve_columns((query_grad, out_grads), lower_bits, position)
    shared = double_rows(activations, lower_bits, position)
    block_rows = query_rows.shape[0]

    def accumulate(running, query_piece, first_group):
        row_start = first_group * block_rows
        columns = lax.dynamic_slice_in_dim(shared, row_start, query_piece.shape[0], 1)
        return running + jnp.dot(columns, query_piece, preferred_element_type=jnp.float32)

    running = accumulate(
        jnp.zeros((shared.shape[0], query_rows.shape[1]), jnp.float32), query_rows, own_group
    )

    def turn_single(turn_index, carried):
        partial_sum, query_piece = carried
        query_piece = shifted(query_piece, "tok", window_size)
        source = (own_group - turn_index - 1) % group_count
        return (accumulate(partial_sum, query_piece, source), query_piece)

    running, unused_piece = lax.fori_loop(0, group_count - 1, turn_single, (running, query_rows))
    partial_value = jnp.sum(running * grad_rows.astype(jnp.float32), axis=1)
    window_tokens = shared.shape[0]
    stored_order = lax.dynamic_slice_in_dim(
        token_order, own_group * window_tokens, window_tokens, 0
    )
    example_of = jnp.take(doc_ids, stored_order)
    example_count = E_DEV * axis_devices
    onehot = (example_of[:, None] == jnp.arange(example_count, dtype=jnp.int32)[None, :]).astype(
        jnp.float32
    )
    example_sums = jnp.dot(partial_value, onehot, precision=lax.Precision.HIGHEST)
    return lax.psum_scatter(example_sums, "tok", scatter_dimension=0, tiled=True)


def solution(mesh):
    placed = (
        P(("groups", "tok"), None),
        P(("groups", "tok"), None),
        P(("groups", "tok"), None),
        P("groups"),
        P("groups"),
    )
    local = on_line if mesh.shape["tok"] == ROW * LINE else per_device
    return jax.shard_map(
        local, mesh=mesh, in_specs=placed, out_specs=P(("groups", "tok")), check_vma=False
    )
```

```python
import functools

import jax
import jax.numpy as jnp
from jax import lax
from jax.experimental import pallas as pl
from jax.experimental.pallas import tpu as pltpu
from jax.sharding import PartitionSpec as P

E_DEV = 2
ROW = 4
LINE = 4
MESH = pl.DeviceIdType.MESH
SPAN = (1, 2, 2, 1)
NEED = ((0,), (0,), (2,), (3,))
RIGHTWARD = {1: (0, 2), 2: (2,), 3: (3,)}
LEFTWARD = {2: (0, 2), 1: (0,), 0: (0,)}


def exchange(
    near, act, grads, query, order, docs, out, g_all, a_all, q_own, q_next, total, mine, slots, final,
    g_recv, a_recv, q_recv, n_recv, row_send, right_a, right_b, left_a, left_b, act_right, act_left,
    act_row, q_send, n_send,
    sum_recv, sum_send,
):
    me = lax.axis_index("tok")
    z = me // ROW
    s = me % ROW
    y, c = s // 2, s % 2
    tokens, features = act.shape
    q_rows = query.shape[0]
    width = g_all.shape[1]
    far = width - near
    block = features // LINE
    core_peer = y * 2 + 1 - c
    y_peer = (1 - y) * 2 + c
    diagonal = (1 - y) * 2 + 1 - c
    peers = (s, core_peer, y_peer, diagonal)

    barrier = pltpu.get_barrier_semaphore()
    for step in range(1, ROW * LINE):
        other = (me + step) % (ROW * LINE)
        pl.semaphore_signal(barrier, inc=1, device_id={"tok": other}, device_id_type=MESH)
    pl.semaphore_wait(barrier, ROW * LINE - 1)

    def remote(source, target, send, recv, line, quarter):
        return pltpu.make_async_remote_copy(
            src_ref=source, dst_ref=target, send_sem=send, recv_sem=recv,
            device_id={"tok": line * ROW + quarter}, device_id_type=MESH,
        )

    def rows(line, quarter):
        return pl.ds(pl.multiple_of((line * ROW + quarter) * tokens, tokens), tokens)

    def g_piece(line, quarter, piece):
        columns = pl.ds(0, near) if piece == 0 else pl.ds(near, far)
        return g_all.at[rows(line, quarter), columns]

    def a_piece(line, quarter, number, target):
        return a_all.at[rows(line, quarter), pl.ds(number * block, SPAN[target] * block)]

    def arrived(ref, sem):
        pltpu.make_async_copy(ref, ref, sem).wait()

    def role(zz, part):
        inner = zz in (1, 2)
        mate = {0: 1, 1: 2, 2: 1, 3: 2}[zz]

        def g_wait(line, quarter, piece):
            arrived(g_piece(line, quarter, piece), g_recv.at[line, quarter, piece])

        def g_forward(line, quarter, piece, target, send):
            ref = g_piece(line, quarter, piece)
            remote(ref, ref, send, g_recv.at[line, quarter, piece], target, s).start()

        def a_wait(line, quarter, number):
            arrived(a_piece(line, quarter, number, zz), a_recv.at[line, quarter, number])

        def a_forward(line, quarter, number, target, target_quarter, send):
            ref = a_piece(line, quarter, number, target)
            remote(ref, ref, send, a_recv.at[line, quarter, number], target, target_quarter).start()

        def q_piece(quarter, piece):
            held = pl.ds(pl.multiple_of(quarter * q_rows, q_rows), q_rows)
            return q_own.at[held, pl.ds(0, near) if piece == 0 else pl.ds(near, far)]

        def q_give(places, piece):
            for place in places:
                quarter = peers[place]
                start = pl.multiple_of(quarter * width + piece * near, 128)
                source = query.at[:, pl.ds(start, far if piece else near)]
                sem = q_recv.at[s, piece]
                if place == 0:
                    pltpu.make_async_copy(source, q_piece(s, piece), sem).start()
                else:
                    remote(source, q_piece(s, piece), q_send, sem, zz, quarter).start()

        def q_take(places, piece):
            for place in places:
                quarter = peers[place]
                arrived(q_piece(quarter, piece), q_recv.at[quarter, piece])
                if piece and not inner:
                    held = pl.ds(pl.multiple_of(quarter * q_rows, q_rows), q_rows)
                    remote(
                        q_piece(quarter, 1), q_next.at[held, :], n_send, n_recv.at[quarter], mate, s
                    ).start()

        def spread(line):
            for number in NEED[zz]:
                for quarter in (core_peer, y_peer):
                    a_forward(line, s, number, zz, quarter, act_row)

        def relay(line):
            for number in NEED[zz]:
                a_wait(line, y_peer, number)
                a_forward(line, y_peer, number, zz, core_peer, act_row)

        def first(zz):
            for place, quarter in enumerate(peers):
                for piece in (0, 1):
                    start = quarter * width + piece * near
                    size = far if piece else near
                    source = grads.at[:, pl.ds(pl.multiple_of(start, 128), size)]
                    target = g_piece(zz, s, piece)
                    sem = g_recv.at[zz, s, piece]
                    if place == 0:
                        pltpu.make_async_copy(source, target, sem).start()
                    else:
                        remote(source, target, row_send, sem, zz, quarter).start()
            for number in NEED[zz]:
                own = act.at[:, pl.ds(number * block, SPAN[zz] * block)]
                pltpu.make_async_copy(own, a_piece(zz, s, number, zz), a_recv.at[zz, s, number]).start()
            for target, numbers, send in (
                (zz + 1, RIGHTWARD.get(zz + 1, ()), act_right), (zz - 1, LEFTWARD.get(zz - 1, ()), act_left),
            ):
                for number in numbers:
                    own = act.at[:, pl.ds(number * block, SPAN[target] * block)]
                    sem = a_recv.at[zz, s, number]
                    remote(own, a_piece(zz, s, number, target), send, sem, target, s).start()

            home(peers[:2])
            for number in NEED[zz]:
                a_wait(zz, s, number)
            spread(zz)

        def home(quarters):
            for quarter in quarters:
                g_wait(zz, quarter, 0)
                if zz < LINE - 1:
                    g_forward(zz, quarter, 0, zz + 1, right_a)
                if zz > 0:
                    g_forward(zz, quarter, 0, zz - 1, left_a)
                g_wait(zz, quarter, 1)
                g_forward(zz, quarter, 1, mate, right_b if zz < 2 else left_b)

        def drain(zz):
            arrived(grads.at[:, pl.ds(0, 3 * width)], row_send)
            arrived(query.at[:, pl.ds(0, 3 * width)], q_send)
            line_rows = ROW * tokens
            if zz < LINE - 1:
                arrived(g_all.at[pl.ds(0, (zz + 1) * line_rows), pl.ds(0, near)], right_a)
                wide = len(RIGHTWARD[zz + 1]) * SPAN[zz + 1] * block
                arrived(a_all.at[pl.ds(0, (zz + 1) * tokens), pl.ds(0, wide)], act_right)
            if zz > 0:
                arrived(g_all.at[pl.ds(0, (LINE - zz) * line_rows), pl.ds(0, near)], left_a)
                wide = len(LEFTWARD[zz - 1]) * SPAN[zz - 1] * block
                arrived(a_all.at[pl.ds(0, (LINE - zz) * tokens), pl.ds(0, wide)], act_left)
            half = g_all.at[pl.ds(0, (2 if inner else 1) * line_rows), pl.ds(near, far)]
            arrived(half, right_b if zz < 2 else left_b)
            if not inner:
                arrived(q_next, n_send)
            wide = SPAN[zz] * block
            arrived(a_all.at[pl.ds(0, 3 * LINE * tokens), pl.ds(0, wide)], act_row)

        last_line = LINE - 1 if zz < 2 else 0
        outside = {1: 0, 2: 3}.get(zz, -1)

        def acts_in(distance):
            from_left, from_right = zz - distance, zz + distance
            if from_left >= 0:
                for number in RIGHTWARD[zz]:
                    a_wait(from_left, s, number)
                for number in RIGHTWARD.get(zz + 1, ()):
                    a_forward(from_left, s, number, zz + 1, s, act_right)
                spread(from_left)
            if from_right < LINE:
                for number in LEFTWARD[zz]:
                    a_wait(from_right, s, number)
                for number in LEFTWARD.get(zz - 1, ()):
                    a_forward(from_right, s, number, zz - 1, s, act_left)
                spread(from_right)

        def grads_in(line, piece, quarters=peers):
            for quarter in quarters:
                g_wait(line, quarter, piece)
                if piece == 0 and line < zz < LINE - 1:
                    g_forward(line, quarter, 0, zz + 1, right_a)
                if piece == 0 and line > zz > 0:
                    g_forward(line, quarter, 0, zz - 1, left_a)
                if piece == 1 and line == outside:
                    g_forward(line, quarter, 1, mate, right_b if zz == 1 else left_b)

        def acts_ready(line):
            for quarter in (core_peer, diagonal):
                for number in NEED[zz]:
                    a_wait(line, quarter, number)

        early_lines = [line for line in range(LINE) if line != last_line]
        if part == 0:
            first(zz)
            acts_in(1)
            home(peers[2:])
            if inner:
                q_give((1, 2, 3, 0), 0)
                acts_in(2)
                q_give((1, 2, 3, 0), 1)
                for quarter in peers:
                    grads_in(mate, 0, (quarter,))
                    grads_in(outside, 0, (quarter,))
                grads_in(outside, 1)
                grads_in(last_line, 0)
                relay(zz)
                relay(mate)
                relay(outside)
                relay(last_line)
                q_take((0, 1, 2, 3), 0)
            else:
                q_give((1, 2, 3, 0), 1)
                q_give((1, 0), 0)
                q_take((0, 1), 1)
                q_take((2, 3), 1)
                acts_in(2)
                q_give((2, 3), 0)
                relay(zz)
                acts_in(3)
                grads_in(mate, 0)
                relay(mate)
                grads_in(3 - mate, 0)
                relay(3 - mate)
                q_take((0, 1, 2, 3), 0)
            for line in early_lines:
                acts_ready(line)
        elif part == 1:
            if not inner:
                grads_in(last_line, 0)
                relay(last_line)
            acts_ready(last_line)
        elif part == 2:
            if inner:
                q_take((0, 1, 2, 3), 1)
                grads_in(mate, 1)
                for quarter in range(ROW):
                    held = pl.ds(quarter * q_rows, q_rows)
                    arrived(q_next.at[held, :], n_recv.at[quarter])
        elif part == 3:
            if inner:
                for quarter in peers[:2]:
                    g_wait(last_line, quarter, 1)
        elif part == 4:
            if inner:
                for quarter in peers[2:]:
                    g_wait(last_line, quarter, 1)
        else:
            drain(zz)

    def run(part):
        for zz in range(LINE):
            pl.when(z == zz)(functools.partial(role, zz, part))

    tall = 2 * tokens
    tile = 512
    is_inner = (z == 1) | (z == 2)
    first_rows = pl.multiple_of((z // 2) * ROW * tokens, tokens)
    last_rows = pl.multiple_of((1 - z // 2) * (LINE - 1) * ROW * tokens, tokens)
    near_act = pl.ds(pl.multiple_of(z * block, block), block)
    mate_line = z + 1 - 2 * (z % 2)
    mate_act = pl.ds(pl.multiple_of(mate_line * block, block), block)

    def add(held, projected, columns):
        weighed = projected * g_all[held, columns].astype(jnp.float32)
        parts = [weighed[:, i * 128 : (i + 1) * 128] for i in range(tile // 128)]
        total[held, :] += sum(parts[1:], parts[0])

    def near_block(start, count):
        def step(number, carried):
            held = pl.ds(pl.multiple_of(start + number % count * tall, tall), tall)
            columns = pl.ds(pl.multiple_of(number // count * tile, tile), tile)
            add(held, jnp.dot(
                a_all[held, near_act], q_own[:, columns], preferred_element_type=jnp.float32
            ), columns)
            return carried

        lax.fori_loop(0, near // tile * count, step, 0)

    def far_block(start, count):
        def step(number, carried):
            held = pl.ds(pl.multiple_of(start + number % count * tall, tall), tall)
            local = pl.multiple_of(number // count * tile, tile)
            columns = pl.ds(pl.multiple_of(near + local, tile), tile)
            projected = jnp.dot(
                a_all[held, near_act], q_own[:, columns], preferred_element_type=jnp.float32
            ) + jnp.dot(
                a_all[held, mate_act], q_next[:, pl.ds(local, tile)],
                preferred_element_type=jnp.float32,
            )
            add(held, projected, columns)
            return carried

        @pl.when(is_inner)
        def _():
            lax.fori_loop(0, far // tile * count, step, 0)

    whole = (LINE - 1) * ROW // 2
    early = pl.multiple_of(last_rows + y * tall, tall)
    late = pl.multiple_of(last_rows + (1 - y) * tall, tall)
    run(0)
    total[...] = jnp.zeros_like(total)
    near_block(first_rows, whole)
    run(1)
    near_block(last_rows, 2)
    run(2)
    far_block(first_rows, whole)
    examples = mine.shape[0]
    numbers = lax.broadcasted_iota(jnp.int32, (examples, order.shape[1]), 0)
    begin = jnp.sum((docs[...] < numbers).astype(jnp.int32), axis=1, keepdims=True)
    end = jnp.sum((docs[...] <= numbers).astype(jnp.int32), axis=1, keepdims=True)

    def example_sums(start, size):
        held = pl.ds(start, size)
        scores = lax.dot_general(
            jnp.ones((8, 128), jnp.float32), total[held, :], (((1,), (1,)), ((), ())),
            precision=lax.Precision.HIGHEST, preferred_element_type=jnp.float32,
        )[0:1, :]
        place = order[:, held]
        member = (place >= begin) & (place < end)
        return jnp.sum(jnp.where(member, scores, 0.0), axis=1, keepdims=True)

    sums = example_sums(first_rows, whole * tall)
    run(3)
    far_block(early, 1)
    sums = sums + example_sums(early, tall)
    run(4)
    far_block(late, 1)
    sums = sums + example_sums(late, tall)

    mine[...] = jnp.broadcast_to(sums, mine.shape)
    slots[me] = mine[...]
    for step in range(1, ROW * LINE):
        other = (me + step) % (ROW * LINE)
        pltpu.make_async_remote_copy(
            src_ref=mine, dst_ref=slots.at[me], send_sem=sum_send, recv_sem=sum_recv.at[me],
            device_id={"tok": other}, device_id_type=MESH,
        ).start()
    for step in range(1, ROW * LINE):
        other = (me + step) % (ROW * LINE)
        arrived(slots.at[other], sum_recv.at[other])
    mine_sum = jnp.sum(slots[...], axis=0)
    final[...] = mine_sum
    out[...] = final[pl.ds(E_DEV * me, E_DEV), :]
    arrived(slots.at[pl.ds(0, ROW * LINE - 1)], sum_send)
    run(5)


def on_line(activations, out_grads, query_grad, token_order, doc_ids):
    tokens, features = activations.shape
    columns = out_grads.shape[1]
    width = columns // ROW
    near = width * 4 // 7 // 256 * 256
    far = width - near
    q_rows = query_grad.shape[0]
    count = ROW * LINE
    dma = pltpu.SemaphoreType.DMA
    examples = E_DEV * count
    vmem = pltpu.VMEM
    sums = pl.pallas_call(
        functools.partial(exchange, near),
        out_shape=jax.ShapeDtypeStruct((E_DEV, 128), jnp.float32),
        in_specs=[pl.BlockSpec(memory_space=pl.ANY)] * 3 + [pl.BlockSpec(memory_space=vmem)] * 2,
        out_specs=pl.BlockSpec(memory_space=vmem),
        scratch_shapes=[
            vmem((count * tokens, width), jnp.bfloat16),
            vmem((count * tokens, features), jnp.bfloat16),
            vmem((ROW * q_rows, width), jnp.bfloat16),
            vmem((ROW * q_rows, far), jnp.bfloat16),
            vmem((count * tokens, 128), jnp.float32),
            vmem((examples, 128), jnp.float32),
            vmem((count, examples, 128), jnp.float32),
            vmem((examples, 128), jnp.float32),
            dma((LINE, ROW, 2)), dma((LINE, ROW, LINE)), dma((ROW, 2)), dma((ROW,)),
        ] + [dma] * 10 + [dma((count,)), dma],
        compiler_params=pltpu.CompilerParams(
            collective_id=0, has_side_effects=True, vmem_limit_bytes=56 * 2**20
        ),
        name="exchange",
    )(
        activations, out_grads, query_grad, token_order.reshape(1, -1), doc_ids.reshape(1, -1)
    )
    return sums[:, 0]


def from_partner(array, axis, bit):
    return lax.ppermute(array, axis, [(i, i ^ 1 << bit) for i in range(lax.axis_size(axis))])


def shifted(value, axis, steps):
    count = lax.axis_size(axis)
    pairs = [(source, (source + steps) % count) for source in range(count)]
    return lax.ppermute(value, axis, pairs)


def order_rows(own_rows, other_rows, own_bit):
    lower_half = jnp.where(own_bit == 0, own_rows, other_rows)
    higher = jnp.where(own_bit == 0, other_rows, own_rows)
    return jnp.concatenate([lower_half, higher], axis=0)


def halve_columns(members, lower_bits, position):
    for bit_number in range(lower_bits):
        own_bit = position >> bit_number & 1
        retained = []
        outgoing = []
        for member in members:
            half_width = member.shape[1] // 2
            retained.append(lax.dynamic_slice_in_dim(member, own_bit * half_width, half_width, 1))
            outgoing.append(
                lax.dynamic_slice_in_dim(member, (1 - own_bit) * half_width, half_width, 1)
            )
        arrived = from_partner((outgoing[0], outgoing[1]), "tok", bit_number)
        members = (
            order_rows(retained[0], arrived[0], own_bit),
            order_rows(retained[1], arrived[1], own_bit),
        )
    return members


def double_rows(activations, lower_bits, position):
    for bit_number in range(lower_bits):
        own_bit = position >> bit_number & 1
        arrived = from_partner(activations, "tok", bit_number)
        activations = order_rows(activations, arrived, own_bit)
    return activations


def per_device(activations, out_grads, query_grad, token_order, doc_ids):
    axis_devices = lax.axis_size("tok")
    position = lax.axis_index("tok")
    lower_bits = 3
    window_size = 2**lower_bits
    group_count = axis_devices // window_size
    own_group = position // window_size
    query_rows, grad_rows = halve_columns((query_grad, out_grads), lower_bits, position)
    shared = double_rows(activations, lower_bits, position)
    block_rows = query_rows.shape[0]

    def accumulate(running, query_piece, first_group):
        row_start = first_group * block_rows
        columns = lax.dynamic_slice_in_dim(shared, row_start, query_piece.shape[0], 1)
        return running + jnp.dot(columns, query_piece, preferred_element_type=jnp.float32)

    running = accumulate(
        jnp.zeros((shared.shape[0], query_rows.shape[1]), jnp.float32), query_rows, own_group
    )

    def turn_single(turn_index, carried):
        partial_sum, query_piece = carried
        query_piece = shifted(query_piece, "tok", window_size)
        source = (own_group - turn_index - 1) % group_count
        return (accumulate(partial_sum, query_piece, source), query_piece)

    running, unused_piece = lax.fori_loop(0, group_count - 1, turn_single, (running, query_rows))
    partial_value = jnp.sum(running * grad_rows.astype(jnp.float32), axis=1)
    window_tokens = shared.shape[0]
    stored_order = lax.dynamic_slice_in_dim(
        token_order, own_group * window_tokens, window_tokens, 0
    )
    example_of = jnp.take(doc_ids, stored_order)
    example_count = E_DEV * axis_devices
    onehot = (example_of[:, None] == jnp.arange(example_count, dtype=jnp.int32)[None, :]).astype(
        jnp.float32
    )
    example_sums = jnp.dot(partial_value, onehot, precision=lax.Precision.HIGHEST)
    return lax.psum_scatter(example_sums, "tok", scatter_dimension=0, tiled=True)


def solution(mesh):
    placed = (
        P(("groups", "tok"), None),
        P(("groups", "tok"), None),
        P(("groups", "tok"), None),
        P("groups"),
        P("groups"),
    )
    local = on_line if mesh.shape["tok"] == ROW * LINE else per_device
    return jax.shard_map(
        local, mesh=mesh, in_specs=placed, out_specs=P(("groups", "tok")), check_vma=False
    )
```
